32 devices in a mesh: replica: 4 (over y, core), expert: 4 (over z), dp: 2 (over x).
Axes of the slice: x: 2, y: 2, z: 4, core: 2. Of those that a mesh axis runs over, the one named last changes fastest.
Arguments:
- tokens: bfloat16 [4, 1024, 3072], P('replica', ('expert', 'dp')), may hold values from -6 to 6
- routes: int32 [4, 1024, 2], P('replica', ('expert', 'dp')), may hold values from 0 to 3, all different within a row; in each aligned block of 128 rows (0 to 127, 128 to 255, ..., all dimensions but the last counted through in order) at most 96 rows name the same one
- route_weight: float32 [4, 1024, 2], P('replica', ('expert', 'dp')), may hold values from 0.1 to 1
- cotangent: bfloat16 [4, 1024, 3072], P('replica', ('expert', 'dp')), may hold values from -6 to 6
- gate_weight: bfloat16 [4, 4, 3072, 512], P('replica', 'expert', None, 'dp'), may hold values from -0.109375 to 0.109375
- up_weight: bfloat16 [4, 4, 3072, 512], P('replica', 'expert', None, 'dp'), may hold values from -0.109375 to 0.109375
- down_weight: bfloat16 [4, 4, 512, 3072], P('replica', 'expert', 'dp'), may hold values from -0.25 to 0.25
- pseudo_grad: float32 [4, 4, 512, 3072], P('replica', 'expert', 'dp'), may hold values from -6 to 6
- anchor: float32 [4, 512, 3072], P('expert', 'dp', 'replica'), may hold values from -6 to 6
- momentum: float32 [4, 512, 3072], P('expert', 'dp', 'replica'), may hold values from -3 to 3
Outputs:
- layer_out: bfloat16 [4, 1024, 3072], P('replica', ('expert', 'dp'))
- mix_grad: float32 [4, 1024, 2], P('replica', ('expert', 'dp'))
- token_grad: bfloat16 [4, 1024, 3072], P('replica', ('expert', 'dp'))
- gate_grad: bfloat16 [4, 4, 3072, 512], P('replica', 'expert', None, 'dp')
- up_grad: bfloat16 [4, 4, 3072, 512], P('replica', 'expert', None, 'dp')
- down_grad: bfloat16 [4, 4, 512, 3072], P('replica', 'expert', 'dp')
- new_anchor: float32 [4, 512, 3072], P('expert', 'dp', 'replica')
- new_momentum: float32 [4, 512, 3072], P('expert', 'dp', 'replica')
The draws below stay inside these ranges and needn't reach their ends.
Inputs may be any that keep to these rules, and one draw needn't show every extreme that they name: `routes`: within the 128 rows of one block no expert is named by more than 96 of the rows, a bound that some block reaches.
All inputs are finite; a program needn't handle non-finite values.
Results may differ from the reference program's by a relative error of at most 0.0072.
Values may be sent and summed in bfloat16 or wider, within the bound.
A program may use at most 192 MiB of HBM per device.

```python
import math
import jax
import jax.numpy as jnp
import numpy as np
from jax import lax

D = 3072
FF_DEV = 256
TOP = 2
TOK_DEV = 128
REPLICAS = 4
EXPERTS = 4
SLABS = 2
FF_SLAB = 512
BLOCKS = 8
TOKENS = 1024
MOST = 96


def levels(own_key, dims, pieces, low, top_value):
    gain, own = 1.0, jax.random.fold_in(own_key, 6)
    for dim, blocks in pieces:
        draws = jnp.exp(jax.random.uniform(jax.random.fold_in(own, dim), (blocks,), jnp.float32, low / len(pieces), top_value / len(pieces)))
        gain = gain * jnp.repeat(draws, dims[dim] // blocks).reshape([-1 if axis == dim else 1 for axis in range(len(dims))])
    return gain


def deal_out(stream_key, own, number, rows, amount, top, bound, slope):
    sequence = jax.random.permutation(stream_key, amount)
    crowded, usual = shares(amount, rows * top, bound, slope, True), shares(amount, rows * top, bound, slope, False)
    places = jnp.arange(amount)

    def named(sizes, rotation):
        used = int((sizes > 0).sum())
        fixed = max(1, used // 4)
        moved = fixed + (places - fixed + rotation * (used - fixed)) % max(1, amount - fixed)
        return jnp.zeros((amount,), jnp.int32).at[sequence[jnp.where(places < fixed, places, moved)]].set(jnp.asarray(sizes, jnp.int32))

    sizes = jnp.where(number % 4 == 0, named(crowded, number // 4), named(usual, number - number // 4 - 1))
    mixed = jax.random.permutation(jax.random.fold_in(own, 3), amount)
    giver, receiver = mixed[0:amount // 2 * 2:2], mixed[1:amount // 2 * 2:2]
    room = jnp.minimum(sizes[giver] - 1, bound - sizes[receiver]) // 2
    room = jnp.where((giver == sequence[0]) | (receiver == sequence[0]) | (sizes[receiver] == 0), 0, jnp.maximum(room, 0))
    moved = jax.random.randint(jax.random.fold_in(own, 4), (amount // 2,), 0, 1 << 20) % (room + 1)
    sizes = sizes.at[giver].add(-moved).at[receiver].add(moved)
    labels = jnp.searchsorted(jnp.cumsum(sizes), jnp.arange(rows * top), side="right").astype(jnp.int32)
    table = labels.reshape(top, rows).T
    table = table[jax.random.permutation(jax.random.fold_in(own, 1), rows)]
    rotation = jax.random.randint(jax.random.fold_in(own, 2), (rows, 1), 0, top)
    return jnp.take_along_axis(table, (jnp.arange(top)[None, :] + rotation) % top, axis=1)


def shares(number_of, total, bound, skew, full):
    loads = [(1 << 20) // math.isqrt(rank ** skew) + 1 for rank in range(1, number_of + 1)]
    largest = bound if full else min(bound, max(-(-total // number_of), total * loads[0] // sum(loads)))
    least = 1 if total - largest >= number_of - 1 else 0
    given, spare = [largest] + [least] * (number_of - 1), total - largest - least * (number_of - 1)
    while spare > 0:
        candidates = [i for i in range(1, number_of) if given[i] < largest] or [i for i in range(1, number_of) if given[i] < bound]
        pool, left = sum([loads[i] for i in candidates]), spare
        for i in candidates:
            more = min(bound - given[i], max(1, left * loads[i] // pool), spare)
            given[i] = given[i] + more
            spare = spare - more
    return np.array(given)


def normal_values(rng, shape, scale, limit, shards=(), kind=jnp.bfloat16):
    drawn = scale * jax.random.normal(rng, shape, jnp.float32)
    if shards:
        drawn = drawn * levels(rng, shape, shards, -0.22, 0.18)
    return jnp.clip(drawn, -limit, limit).astype(kind)


def setup_inputs(seed: int = 0) -> dict:
    seeds = jax.random.split(jax.random.key(seed), 11)
    tokens = normal_values(seeds[0], (REPLICAS, TOKENS, D), 1.0, 6.0, ((0, 4), (1, 8)))
    routes_keys = jax.random.split(jax.random.fold_in(seeds[1], 1), REPLICAS * TOKENS // TOK_DEV)
    routes_turns = jax.random.permutation(jax.random.fold_in(seeds[1], 3), REPLICAS * TOKENS // TOK_DEV)
    routes = jax.vmap(lambda own, number: deal_out(jax.random.fold_in(seeds[1], 2), own, number, TOK_DEV, EXPERTS, TOP, MOST, 3))(routes_keys, routes_turns).reshape((REPLICAS, TOKENS, TOP))
    route_weight = jnp.clip(jnp.exp(math.log(1.0) - 2.3025851 * jax.random.uniform(seeds[2], (REPLICAS, TOKENS, TOP), jnp.float32) ** levels(seeds[2], (REPLICAS, TOKENS, TOP), ((0, 4), (1, 8)), -0.2, 0.2)), 0.1, 1.0)
    cotangent = normal_values(seeds[3], (REPLICAS, TOKENS, D), 1.0, 6.0, ((0, 4), (1, 8)))
    gate_weight = normal_values(seeds[4], (REPLICAS, EXPERTS, D, FF_SLAB), D ** -0.5, 0.109375, ((0, 4), (1, 4), (3, 2)))
    up_weight = normal_values(seeds[5], (REPLICAS, EXPERTS, D, FF_SLAB), D ** -0.5, 0.109375, ((0, 4), (1, 4), (3, 2)))
    down_weight = normal_values(seeds[6], (REPLICAS, EXPERTS, FF_SLAB, D), FF_SLAB ** -0.5, 0.25, ((0, 4), (1, 4), (2, 2)))
    pseudo_grad = normal_values(seeds[7], (REPLICAS, EXPERTS, FF_SLAB, D), 1.0, 6.0, ((0, 4), (1, 4), (2, 2)), jnp.float32)
    anchor = normal_values(seeds[8], (EXPERTS, FF_SLAB, D), 1.0, 6.0, ((0, 4), (1, 2), (2, 4)), jnp.float32)
    momentum = normal_values(seeds[9], (EXPERTS, FF_SLAB, D), 0.5, 3.0, ((0, 4), (1, 2), (2, 4)), jnp.float32)
    return dict(tokens=tokens, routes=routes, route_weight=route_weight, cotangent=cotangent, gate_weight=gate_weight, up_weight=up_weight, down_weight=down_weight, pseudo_grad=pseudo_grad, anchor=anchor, momentum=momentum)


OUTER_MU = 0.9
OUTER_RATE = 0.7


def rounded(value):
    return lax.optimization_barrier(value.astype(jnp.bfloat16)).astype(jnp.float32)


def destinations(choice_ids, experts, capacity):
    flat_ids = choice_ids.reshape(-1)
    onehot = (flat_ids[:, None] == jnp.arange(experts, dtype=jnp.int32)[None, :]).astype(jnp.int32)
    counts = jnp.cumsum(onehot, axis=0)
    rank_slot = jnp.sum(counts * onehot, axis=1) - 1
    return (flat_ids * capacity + rank_slot).reshape(choice_ids.shape).astype(jnp.int32)


def silu_parts(gate_pre):
    sigmoid_gate = jax.nn.sigmoid(gate_pre)
    return gate_pre * sigmoid_gate, sigmoid_gate * (1.0 + gate_pre * (1.0 - sigmoid_gate))


def block_slots(choice_ids):
    return destinations(choice_ids, EXPERTS, MOST)


def place_rows(row_values, slot_dest):
    buffer = jnp.zeros((EXPERTS * MOST, D), row_values.dtype)
    return buffer.at[slot_dest.reshape(-1)].set(row_values.reshape(-1, D))


def take_rows(rows_all, slot_dest):
    return jnp.take(rows_all, slot_dest.reshape(-1), axis=0)


def expert_step(operands):
    rows_in, rows_cot, gate_w, up_w, down_w = operands
    flat_in = rows_in.reshape(-1, D)
    flat_cot = rows_cot.reshape(-1, D)
    gate_pre = jnp.dot(flat_in, gate_w, preferred_element_type=jnp.float32)
    up_pre = jnp.dot(flat_in, up_w, preferred_element_type=jnp.float32)
    silu_gate, silu_slope = silu_parts(gate_pre)
    hidden = (silu_gate * up_pre).astype(jnp.bfloat16)
    hidden_slabs = hidden.reshape(-1, SLABS, FF_DEV).astype(jnp.float32)
    y_parts = jnp.einsum("rjf,jfd->jrd", hidden_slabs, down_w.reshape(SLABS, FF_DEV, D).astype(jnp.float32))
    expert_out = jnp.sum(rounded(y_parts), axis=0).astype(jnp.bfloat16)
    back_hidden = jnp.dot(flat_cot, down_w.T, preferred_element_type=jnp.float32)
    gate_delta = (back_hidden * up_pre * silu_slope).astype(jnp.bfloat16)
    up_delta = (back_hidden * silu_gate).astype(jnp.bfloat16)
    dx_parts = jnp.einsum("rjf,djf->jrd", gate_delta.reshape(-1, SLABS, FF_DEV).astype(jnp.float32),
                          gate_w.reshape(D, SLABS, FF_DEV).astype(jnp.float32))
    dx_parts = dx_parts + jnp.einsum("rjf,djf->jrd", up_delta.reshape(-1, SLABS, FF_DEV).astype(jnp.float32),
                                     up_w.reshape(D, SLABS, FF_DEV).astype(jnp.float32))
    expert_dx = jnp.sum(rounded(dx_parts), axis=0).astype(jnp.bfloat16)
    owners = BLOCKS // SLABS
    in_groups = rows_in.reshape(owners, SLABS, MOST, D).astype(jnp.float32)
    cot_groups = rows_cot.reshape(owners, SLABS, MOST, D).astype(jnp.float32)
    gate_groups = gate_delta.reshape(owners, SLABS, MOST, FF_SLAB).astype(jnp.float32)
    up_groups = up_delta.reshape(owners, SLABS, MOST, FF_SLAB).astype(jnp.float32)
    hidden_groups = hidden.reshape(owners, SLABS, MOST, FF_SLAB).astype(jnp.float32)
    gate_grad = jnp.sum(rounded(jnp.einsum("abmd,abmf->bdf", in_groups, gate_groups)), axis=0).astype(jnp.bfloat16)
    up_grad = jnp.sum(rounded(jnp.einsum("abmd,abmf->bdf", in_groups, up_groups)), axis=0).astype(jnp.bfloat16)
    down_grad = jnp.sum(rounded(jnp.einsum("abmf,abmd->bfd", hidden_groups, cot_groups)), axis=0).astype(jnp.bfloat16)
    return (expert_out.reshape(BLOCKS, MOST, D), expert_dx.reshape(BLOCKS, MOST, D), gate_grad, up_grad, down_grad)


def island(operands):
    tokens, routes, route_weight, cotangent, gate_weight, up_weight, down_weight = operands
    slot_dest = jax.vmap(block_slots)(routes.reshape(BLOCKS, TOK_DEV, TOP))
    copies = jnp.broadcast_to(tokens.reshape(BLOCKS, TOK_DEV, 1, D), (BLOCKS, TOK_DEV, TOP, D))
    mix_weight = route_weight.reshape(BLOCKS, TOK_DEV, TOP)
    cot_blocks = cotangent.reshape(BLOCKS, TOK_DEV, 1, D).astype(jnp.float32)
    scaled_cot = (mix_weight[:, :, :, None] * cot_blocks).astype(jnp.bfloat16)
    expert_in = jax.vmap(place_rows)(copies, slot_dest).reshape(BLOCKS, EXPERTS, MOST, D).transpose(1, 0, 2, 3)
    expert_cot = jax.vmap(place_rows)(scaled_cot, slot_dest).reshape(BLOCKS, EXPERTS, MOST, D).transpose(1, 0, 2, 3)
    expert_out, expert_dx, gate_grad, up_grad, down_grad = lax.map(
        expert_step, (expert_in, expert_cot, gate_weight, up_weight, down_weight))
    out_rows = expert_out.transpose(1, 0, 2, 3).reshape(BLOCKS, EXPERTS * MOST, D)
    dx_rows = expert_dx.transpose(1, 0, 2, 3).reshape(BLOCKS, EXPERTS * MOST, D)
    picked = jax.vmap(take_rows)(out_rows, slot_dest).reshape(BLOCKS, TOK_DEV, TOP, D).astype(jnp.float32)
    picked_dx = jax.vmap(take_rows)(dx_rows, slot_dest).reshape(BLOCKS, TOK_DEV, TOP, D).astype(jnp.float32)
    layer_out = jnp.sum(picked * mix_weight[:, :, :, None], axis=2).astype(jnp.bfloat16).reshape(TOKENS, D)
    mix_grad = jnp.sum(picked * cot_blocks, axis=3).reshape(TOKENS, TOP)
    token_grad = jnp.sum(picked_dx, axis=2).astype(jnp.bfloat16).reshape(TOKENS, D)
    return (layer_out, mix_grad, token_grad, gate_grad, up_grad, down_grad)


def reference(tokens, routes, route_weight, cotangent, gate_weight, up_weight, down_weight, pseudo_grad, anchor, momentum):
    layer_out, mix_grad, token_grad, gate_grad, up_grad, down_grad = lax.map(
        island, (tokens, routes, route_weight, cotangent, gate_weight, up_weight, down_weight))
    mean_grad = jnp.sum(pseudo_grad, axis=0) / REPLICAS
    new_momentum = OUTER_MU * momentum + mean_grad
    new_anchor = anchor - OUTER_RATE * (mean_grad + OUTER_MU * new_momentum)
    return (layer_out, mix_grad, token_grad, gate_grad, up_grad, down_grad, new_anchor, new_momentum)
```

```python
import functools

import jax
import jax.numpy as jnp
from jax import lax
from jax.experimental import pallas as pl
from jax.experimental.pallas import tpu as pltpu
from jax.sharding import PartitionSpec as P

OUTER_MU = 0.9
OUTER_RATE = 0.7


def contract_last(left, right):
    return lax.dot_general(
        left, right, (((1,), (1,)), ((), ())), preferred_element_type=jnp.float32
    )


def contract_first(left, right):
    return lax.dot_general(
        left, right, (((0,), (0,)), ((), ())), preferred_element_type=jnp.float32
    )


MESH = pl.DeviceIdType.MESH
VMEM_BYTES = 58 * 2**20
CHUNK = 16


def enter(levels):
    e, x = lax.axis_index("expert"), lax.axis_index("dp")
    barrier = pltpu.get_barrier_semaphore()
    pl.semaphore_signal(barrier, inc=1, device_id={"dp": 1 - x}, device_id_type=MESH)

    @pl.when(e > 0)
    def _():
        pl.semaphore_signal(barrier, inc=1, device_id={"expert": e - 1}, device_id_type=MESH)

    @pl.when(e < levels - 1)
    def _():
        pl.semaphore_signal(barrier, inc=1, device_id={"expert": e + 1}, device_id_type=MESH)

    at_end = (e == 0) | (e == levels - 1)

    @pl.when(at_end)
    def _():
        pl.semaphore_wait(barrier, 2)

    @pl.when(jnp.logical_not(at_end))
    def _():
        pl.semaphore_wait(barrier, 3)


def remote(src, dst, sems, device):
    return pltpu.make_async_remote_copy(
        src_ref=src, dst_ref=dst, send_sem=sems[0], recv_sem=sems[1], device_id=device, device_id_type=MESH
    )


def gather_kernel(levels, tok, cot, tok_all, cot_all, own_sem, z_send, z_recv, x_send, x_recv, ex_send, ex_recv):
    e, x = lax.axis_index("expert"), lax.axis_index("dp")
    last = levels - 1
    mine, full = (tok, cot), (tok_all, cot_all)
    pos = (e, last - e)
    sign = (-1, 1)
    enter(levels)
    local = [pltpu.make_async_copy(mine[a], full[a].at[e, x], own_sem.at[a]) for a in range(2)]
    for copy in local:
        copy.start()

    def z_copy(d, k, a):
        level = e + sign[d] * (k - 1)
        src = mine[a] if k == 1 else full[a].at[level, x]
        return remote(src, full[a].at[level, x], (z_send.at[d, k, a], z_recv.at[d, k, a]), {"expert": e - sign[d]})

    def z_in(d, k, a):
        level = e + sign[d] * k
        ref = full[a].at[level, x]
        return remote(ref, ref, (z_send.at[d, k, a], z_recv.at[d, k, a]), {"expert": e + sign[d]})

    def x_copy(d, k, a):
        level = e + sign[d] * k
        src = mine[a] if k == 0 else full[a].at[level, x]
        return remote(src, full[a].at[level, x], (x_send.at[d, k, a], x_recv.at[d, k, a]), {"dp": 1 - x})

    def x_in(d, k, a):
        ref = full[a].at[e + sign[d] * k, 1 - x]
        return remote(ref, ref, (x_send.at[d, k, a], x_recv.at[d, k, a]), {"dp": 1 - x})

    def ex_copy(d, go):
        ref = cot_all.at[0 if d == 0 else last, 1 - x]
        return remote(ref, ref, (ex_send.at[d], ex_recv.at[d]), {"expert": e - sign[d] if go else e + sign[d]})

    def crosses(d, k, a):
        return pos[d] > k if a == 1 else pos[d] >= k

    for a in range(2):
        x_copy(0, 0, a).start()
        for d in range(2):
            @pl.when(pos[d] < last)
            def _(d=d, a=a):
                z_copy(d, 1, a).start()

    for k in range(1, levels):
        for a in range(2):
            for d in range(2):
                @pl.when(pos[d] >= k)
                def _(d=d, k=k, a=a):
                    z_in(d, k, a).wait_recv()

                    if k < last:
                        @pl.when(pos[d] < last)
                        def _():
                            z_copy(d, k + 1, a).start()

                @pl.when(crosses(d, k, a))
                def _(d=d, k=k, a=a):
                    x_copy(d, k, a).start()

        if k == 1:
            x_in(0, 0, 1).wait_recv()
            for d in range(2):
                @pl.when(pos[d] == 0)
                def _(d=d):
                    ex_copy(d, True).start()

        for d in range(2):
            @pl.when(pos[d] == k)
            def _(d=d):
                ex_copy(d, False).wait_recv()

                @pl.when(pos[d] < last)
                def _():
                    ex_copy(d, True).start()

    x_in(0, 0, 0).wait_recv()
    for a in range(2):
        x_copy(0, 0, a).wait_send()
    for k in range(1, levels):
        for a in range(2):
            for d in range(2):
                @pl.when(crosses(d, k, a))
                def _(d=d, k=k, a=a):
                    x_in(d, k, a).wait_recv()
                    x_copy(d, k, a).wait_send()

                @pl.when((pos[d] < last) & (pos[d] >= k - 1))
                def _(d=d, k=k, a=a):
                    z_copy(d, k, a).wait_send()

    for d in range(2):
        @pl.when(pos[d] < last)
        def _(d=d):
            ex_copy(d, True).wait_send()
    for copy in local:
        copy.wait()


def scatter_kernel(
    levels, y, dx, y_out, dx_out, held, zbuf, ex, z_send, z_recv, x_send, x_recv, ex_send, ex_recv
):
    e, x = lax.axis_index("expert"), lax.axis_index("dp")
    last = levels - 1
    part, outs = (y, dx), (y_out, dx_out)
    pos = (e, last - e)
    sign = (-1, 1)
    rows = y.shape[2]
    enter(levels)

    def add(dst, srcs):
        def body(i, carry):
            at = pl.ds(pl.multiple_of(i * CHUNK, CHUNK), CHUNK)
            total = srcs[0][at, :].astype(jnp.float32)
            for src in srcs[1:]:
                total = total + src[at, :].astype(jnp.float32)
            dst[at, :] = total.astype(dst.dtype)
            return carry

        lax.fori_loop(0, rows // CHUNK, body, 0)

    def owner(d, k):
        return e + sign[d] * k

    def x_copy(d, k, a, src=None):
        s = owner(d, k)
        src = part[a].at[s, 1 - x] if src is None else src
        return remote(src, held.at[a, s], (x_send.at[d, k, a], x_recv.at[d, k, a]), {"dp": 1 - x})

    def z_copy(d, k, a):
        s = owner(d, k)
        return remote(held.at[a, s], zbuf.at[d, a, s], (z_send.at[d, k, a], z_recv.at[d, k, a]), {"expert": e + sign[d]})

    def z_in(d, k, a):
        ref = zbuf.at[d, a, owner(d, k)]
        return remote(ref, ref, (z_send.at[d, k + 1, a], z_recv.at[d, k + 1, a]), {"expert": e - sign[d]})

    def ex_copy(d):
        end = 0 if d == 0 else last
        return remote(ex.at[d], ex.at[2 + d], (ex_send.at[d], ex_recv.at[d]), {"expert": e + sign[d]})

    def crosses(d, k, a):
        return pos[d] > k if a == 1 else pos[d] >= k

    at_end = (e == 0) | (e == last)

    for d in range(2):
        end = 0 if d == 0 else last

        @pl.when(pos[d] == last)
        def _(d=d, end=end):
            add(ex.at[d], [dx.at[end, 1 - x]])
            ex_copy(d).start()

    for k in range(last, 0, -1):
        for a in range(2):
            for d in range(2):
                @pl.when(crosses(d, k, a))
                def _(d=d, k=k, a=a):
                    x_copy(d, k, a).start()
    x_copy(0, 0, 0).start()

    @pl.when(jnp.logical_not(at_end))
    def _():
        x_copy(0, 0, 1).start()

    for k in range(last, 0, -1):
        for a in (1, 0):
            for d in range(2):
                @pl.when(pos[d] >= k)
                def _(d=d, k=k, a=a):
                    s = owner(d, k)
                    own = part[a].at[s, x]
                    slot = held.at[a, s]

                    def ready(crossed):
                        if k < last:
                            @pl.when(pos[d] < last)
                            def _():
                                z_in(d, k, a).wait_recv()
                                add(slot, [own, zbuf.at[d, a, s]] + ([slot] if crossed else []))

                        @pl.when(pos[d] == last)
                        def _():
                            add(slot, [own] + ([slot] if crossed else []))

                    if a == 0:
                        x_copy(d, k, a).wait_recv()
                        ready(True)
                    else:
                        @pl.when(pos[d] > k)
                        def _():
                            x_copy(d, k, a).wait_recv()
                            ready(True)

                        @pl.when(pos[d] == k)
                        def _():
                            ready(False)
                    z_copy(d, k, a).start()

        for d in range(2):
            end = 0 if d == 0 else last

            @pl.when(pos[d] == k - 1)
            def _(d=d, end=end, k=k):
                ex_copy(d).wait_recv()
                add(ex.at[d], [ex.at[2 + d], dx.at[end, 1 - x]])
                if k > 1:
                    ex_copy(d).start()
                else:
                    x_copy(0, 0, 1, ex.at[d]).start()

    for a in range(2):
        x_copy(0, 0, a).wait_recv()
        near = [part[a].at[e, x], held.at[a, e]]

        @pl.when(e < last)
        def _(a=a):
            z_in(0, 0, a).wait_recv()

        @pl.when(e > 0)
        def _(a=a):
            z_in(1, 0, a).wait_recv()

        @pl.when(e == 0)
        def _(a=a, near=near):
            add(outs[a], near + [zbuf.at[0, a, e]])

        @pl.when(e == last)
        def _(a=a, near=near):
            add(outs[a], near + [zbuf.at[1, a, e]])

        @pl.when(jnp.logical_not(at_end))
        def _(a=a, near=near):
            add(outs[a], near + [zbuf.at[0, a, e], zbuf.at[1, a, e]])

    for a in range(2):
        x_copy(0, 0, a).wait_send()
        for k in range(1, levels):
            for d in range(2):
                @pl.when(crosses(d, k, a))
                def _(d=d, k=k, a=a):
                    x_copy(d, k, a).wait_send()

                @pl.when(pos[d] >= k)
                def _(d=d, k=k, a=a):
                    z_copy(d, k, a).wait_send()

    for d in range(2):
        @pl.when(pos[d] > 0)
        def _(d=d):
            ex_copy(d).wait_send()


def sems(levels):
    shape = (2, levels + 1, 2)
    return [pltpu.SemaphoreType.DMA(shape)] * 4 + [pltpu.SemaphoreType.DMA((2,))] * 2


def gather_rows(tok, cot, levels, lines):
    if not by_kernel(tok.shape, levels, lines):
        return tuple(lax.all_gather(v, ("expert", "dp"), axis=0, tiled=True) for v in (tok, cot))
    full = jax.ShapeDtypeStruct((levels, lines) + tok.shape, tok.dtype)
    got = pl.pallas_call(
        functools.partial(gather_kernel, levels),
        out_shape=(full, full),
        in_specs=[pl.BlockSpec(memory_space=pl.ANY)] * 2,
        out_specs=(pl.BlockSpec(memory_space=pl.ANY),) * 2,
        scratch_shapes=[pltpu.SemaphoreType.DMA((2,))] + sems(levels),
        compiler_params=pltpu.CompilerParams(collective_id=0, has_side_effects=True),
    )(tok, cot)
    return tuple(v.reshape(-1, tok.shape[1]) for v in got)


def scatter_sums(y_part, dx_part, levels, lines):
    width = y_part.shape[1]
    rows = y_part.shape[0] // (levels * lines)
    if not by_kernel((rows, width), levels, lines):
        return tuple(
            lax.psum_scatter(v, ("expert", "dp"), scatter_dimension=0, tiled=True) for v in (y_part, dx_part)
        )
    one = jax.ShapeDtypeStruct((rows, width), y_part.dtype)
    vmem = pl.BlockSpec(memory_space=pltpu.VMEM)
    return pl.pallas_call(
        functools.partial(scatter_kernel, levels),
        out_shape=(one, one),
        in_specs=[vmem] * 2,
        out_specs=(vmem,) * 2,
        scratch_shapes=[
            pltpu.VMEM((2, levels, rows, width), y_part.dtype),
            pltpu.VMEM((2, 2, levels, rows, width), y_part.dtype),
            pltpu.VMEM((4, rows, width), y_part.dtype),
        ]
        + sems(levels),
        compiler_params=pltpu.CompilerParams(
            collective_id=1, has_side_effects=True, vmem_limit_bytes=VMEM_BYTES
        ),
    )(
        y_part.reshape(levels, lines, rows, width), dx_part.reshape(levels, lines, rows, width)
    )


def by_kernel(block, levels, lines):
    rows, width = block
    blocks = 2 * levels * lines + 6 * levels + 6
    return lines == 2 and levels > 2 and rows % CHUNK == 0 and 2 * blocks * rows * width < VMEM_BYTES


def shards(
    tokens,
    routes,
    route_weight,
    cotangent,
    gate_weight,
    up_weight,
    down_weight,
    pseudo_grad,
    anchor,
    momentum,
):
    axes = ("expert", "dp")
    me = lax.axis_index("expert")
    levels, lines = lax.axis_size("expert"), lax.axis_size("dp")
    tok, cot = gather_rows(tokens[0], cotangent[0], levels, lines)
    ids = lax.all_gather(routes[0].T, axes, axis=1, tiled=True)
    wts = lax.all_gather(route_weight[0].T, axes, axis=1, tiled=True)
    hit = ids == me
    weight = jnp.sum(jnp.where(hit, wts, 0.0), axis=0)[:, None]
    gate_w = gate_weight[0, 0]
    up_w = up_weight[0, 0]
    down_w = down_weight[0, 0]

    gate_pre = jnp.dot(tok, gate_w, preferred_element_type=jnp.float32)
    up_pre = jnp.dot(tok, up_w, preferred_element_type=jnp.float32)
    sig = jax.nn.sigmoid(gate_pre)
    silu_gate = gate_pre * sig
    hidden = silu_gate * up_pre
    hidden_w = (hidden * weight).astype(jnp.bfloat16)
    y_part = jnp.dot(hidden_w, down_w, preferred_element_type=jnp.float32).astype(jnp.bfloat16)

    back = contract_last(cot, down_w)
    mix_rows = jnp.sum(hidden * back, axis=1)
    back_w = back * weight
    gate_delta = (back_w * up_pre * (sig * (1.0 + gate_pre * (1.0 - sig)))).astype(jnp.bfloat16)
    up_delta = (back_w * silu_gate).astype(jnp.bfloat16)
    dx_part = (contract_last(gate_delta, gate_w) + contract_last(up_delta, up_w)).astype(jnp.bfloat16)
    layer_out, token_grad = scatter_sums(y_part, dx_part, levels, lines)
    mix_part = jnp.where(hit, mix_rows[None, :], 0.0)
    mix_grad = lax.psum_scatter(mix_part, axes, scatter_dimension=1, tiled=True).T

    gate_grad = contract_first(tok, gate_delta).astype(jnp.bfloat16)
    up_grad = contract_first(tok, up_delta).astype(jnp.bfloat16)
    down_grad = contract_first(hidden_w, cot).astype(jnp.bfloat16)

    island_count = lax.axis_size("replica")
    summed = lax.psum_scatter(
        pseudo_grad[0, 0].astype(jnp.bfloat16), "replica", scatter_dimension=1, tiled=True
    ).astype(jnp.float32)
    mean_grad = summed / island_count
    new_momentum = OUTER_MU * momentum[0] + mean_grad
    new_anchor = anchor[0] - OUTER_RATE * (mean_grad + OUTER_MU * new_momentum)
    return (
        layer_out[None],
        mix_grad[None],
        token_grad[None],
        gate_grad[None, None],
        up_grad[None, None],
        down_grad[None, None],
        new_anchor[None],
        new_momentum[None],
    )


ROWS = P("replica", ("expert", "dp"), None)
COLS = P("replica", "expert", None, "dp")
HIDS = P("replica", "expert", "dp", None)
OUTER = P("expert", "dp", "replica")


def solution(mesh):
    return jax.shard_map(
        shards,
        mesh=mesh,
        in_specs=(ROWS, ROWS, ROWS, ROWS, COLS, COLS, HIDS, HIDS, OUTER, OUTER),
        out_specs=(ROWS, ROWS, ROWS, COLS, COLS, HIDS, OUTER, OUTER),
        check_vma=False,
    )
```

```python
import functools

import jax
import jax.numpy as jnp
from jax import lax
from jax.experimental import pallas as pl
from jax.experimental.pallas import tpu as pltpu
from jax.sharding import PartitionSpec as P

OUTER_MU = 0.9
OUTER_RATE = 0.7


def contract_last(left, right):
    return lax.dot_general(
        left, right, (((1,), (1,)), ((), ())), preferred_element_type=jnp.float32
    )


def contract_first(left, right):
    return lax.dot_general(
        left, right, (((0,), (0,)), ((), ())), preferred_element_type=jnp.float32
    )


MESH = pl.DeviceIdType.MESH
VMEM_BYTES = 58 * 2**20
CHUNK = 16
TILE = 256


def enter(levels):
    e, x = lax.axis_index("expert"), lax.axis_index("dp")
    barrier = pltpu.get_barrier_semaphore()
    pl.semaphore_signal(barrier, inc=1, device_id={"dp": 1 - x}, device_id_type=MESH)

    @pl.when(e > 0)
    def _():
        pl.semaphore_signal(barrier, inc=1, device_id={"expert": e - 1}, device_id_type=MESH)

    @pl.when(e < levels - 1)
    def _():
        pl.semaphore_signal(barrier, inc=1, device_id={"expert": e + 1}, device_id_type=MESH)

    at_end = (e == 0) | (e == levels - 1)

    @pl.when(at_end)
    def _():
        pl.semaphore_wait(barrier, 2)

    @pl.when(jnp.logical_not(at_end))
    def _():
        pl.semaphore_wait(barrier, 3)


def remote(src, dst, sems, device):
    return pltpu.make_async_remote_copy(
        src_ref=src, dst_ref=dst, send_sem=sems[0], recv_sem=sems[1], device_id=device, device_id_type=MESH
    )


def gather_kernel(levels, tok, cot, meta, tok_all, cot_all, meta_all, own_sem, z_send, z_recv, x_send, x_recv, ex_send, ex_recv):
    e, x = lax.axis_index("expert"), lax.axis_index("dp")
    last = levels - 1
    mine, full = (tok, cot, meta), (tok_all, cot_all, meta_all)
    order = (2, 0, 1)
    pos = (e, last - e)
    sign = (-1, 1)
    enter(levels)
    local = [pltpu.make_async_copy(mine[a], full[a].at[e, x], own_sem.at[a]) for a in order]
    for copy in local:
        copy.start()

    def z_copy(d, k, a):
        level = e + sign[d] * (k - 1)
        src = mine[a] if k == 1 else full[a].at[level, x]
        return remote(src, full[a].at[level, x], (z_send.at[d, k, a], z_recv.at[d, k, a]), {"expert": e - sign[d]})

    def z_in(d, k, a):
        level = e + sign[d] * k
        ref = full[a].at[level, x]
        return remote(ref, ref, (z_send.at[d, k, a], z_recv.at[d, k, a]), {"expert": e + sign[d]})

    def x_copy(d, k, a):
        level = e + sign[d] * k
        src = mine[a] if k == 0 else full[a].at[level, x]
        return remote(src, full[a].at[level, x], (x_send.at[d, k, a], x_recv.at[d, k, a]), {"dp": 1 - x})

    def x_in(d, k, a):
        ref = full[a].at[e + sign[d] * k, 1 - x]
        return remote(ref, ref, (x_send.at[d, k, a], x_recv.at[d, k, a]), {"dp": 1 - x})

    def ex_copy(d, go):
        ref = cot_all.at[0 if d == 0 else last, 1 - x]
        return remote(ref, ref, (ex_send.at[d], ex_recv.at[d]), {"expert": e - sign[d] if go else e + sign[d]})

    def crosses(d, k, a):
        return pos[d] > k if a == 1 else pos[d] >= k

    for a in order:
        x_copy(0, 0, a).start()
        for d in range(2):
            @pl.when(pos[d] < last)
            def _(d=d, a=a):
                z_copy(d, 1, a).start()

    for k in range(1, levels):
        for a in order:
            for d in range(2):
                @pl.when(pos[d] >= k)
                def _(d=d, k=k, a=a):
                    z_in(d, k, a).wait_recv()

                    if k < last:
                        @pl.when(pos[d] < last)
                        def _():
                            z_copy(d, k + 1, a).start()

                @pl.when(crosses(d, k, a))
                def _(d=d, k=k, a=a):
                    x_copy(d, k, a).start()

        if k == 1:
            x_in(0, 0, 1).wait_recv()
            for d in range(2):
                @pl.when(pos[d] == 0)
                def _(d=d):
                    ex_copy(d, True).start()

        for d in range(2):
            @pl.when(pos[d] == k)
            def _(d=d):
                ex_copy(d, False).wait_recv()

                @pl.when(pos[d] < last)
                def _():
                    ex_copy(d, True).start()

    x_in(0, 0, 0).wait_recv()
    x_in(0, 0, 2).wait_recv()
    for a in order:
        x_copy(0, 0, a).wait_send()
    for k in range(1, levels):
        for a in order:
            for d in range(2):
                @pl.when(crosses(d, k, a))
                def _(d=d, k=k, a=a):
                    x_in(d, k, a).wait_recv()
                    x_copy(d, k, a).wait_send()

                @pl.when((pos[d] < last) & (pos[d] >= k - 1))
                def _(d=d, k=k, a=a):
                    z_copy(d, k, a).wait_send()

    for d in range(2):
        @pl.when(pos[d] < last)
        def _(d=d):
            ex_copy(d, True).wait_send()
    for copy in local:
        copy.wait()


def scatter_kernel(
    levels,
    y,
    dx,
    gate_delta,
    up_delta,
    hidden_w,
    tok_hbm,
    cot_hbm,
    y_out,
    dx_out,
    gate_hbm,
    up_hbm,
    down_hbm,
    held,
    zbuf,
    ex,
    tok,
    cot,
    gate_grad,
    up_grad,
    down_grad,
    load_sem,
    store_sem,
    z_send,
    z_recv,
    x_send,
    x_recv,
    ex_send,
    ex_recv,
):
    e, x = lax.axis_index("expert"), lax.axis_index("dp")
    last = levels - 1
    part, outs = (y, dx), (y_out, dx_out)
    pos = (e, last - e)
    sign = (-1, 1)
    rows = y.shape[2]
    loads = [pltpu.make_async_copy(tok_hbm, tok, load_sem.at[0]), pltpu.make_async_copy(cot_hbm, cot, load_sem.at[1])]
    for copy in loads:
        copy.start()
    enter(levels)
    tiles = tok.shape[1] // TILE
    slots = 2 * last

    def contract(left, right):
        return contract_first(left, right).astype(jnp.bfloat16)

    def gradients(slot):
        def body(i, carry):
            at = pl.ds(pl.multiple_of(i * TILE, TILE), TILE)
            gate_grad[at, :] = contract(tok[:, at], gate_delta[...])
            up_grad[at, :] = contract(tok[:, at], up_delta[...])
            down_grad[:, at] = contract(hidden_w[...], cot[:, at])
            return carry

        lax.fori_loop(slot * tiles // slots, (slot + 1) * tiles // slots, body, 0)

    def add(dst, srcs):
        def body(i, carry):
            at = pl.ds(pl.multiple_of(i * CHUNK, CHUNK), CHUNK)
            total = srcs[0][at, :].astype(jnp.float32)
            for src in srcs[1:]:
                total = total + src[at, :].astype(jnp.float32)
            dst[at, :] = total.astype(dst.dtype)
            return carry

        lax.fori_loop(0, rows // CHUNK, body, 0)

    def owner(d, k):
        return e + sign[d] * k

    def x_copy(d, k, a, src=None):
        s = owner(d, k)
        src = part[a].at[s, 1 - x] if src is None else src
        return remote(src, held.at[a, s], (x_send.at[d, k, a], x_recv.at[d, k, a]), {"dp": 1 - x})

    def z_copy(d, k, a):
        s = owner(d, k)
        return remote(held.at[a, s], zbuf.at[d, a, s], (z_send.at[d, k, a], z_recv.at[d, k, a]), {"expert": e + sign[d]})

    def z_in(d, k, a):
        ref = zbuf.at[d, a, owner(d, k)]
        return remote(ref, ref, (z_send.at[d, k + 1, a], z_recv.at[d, k + 1, a]), {"expert": e - sign[d]})

    def ex_copy(d):
        end = 0 if d == 0 else last
        return remote(ex.at[d], ex.at[2 + d], (ex_send.at[d], ex_recv.at[d]), {"expert": e + sign[d]})

    def crosses(d, k, a):
        return pos[d] > k if a == 1 else pos[d] >= k

    at_end = (e == 0) | (e == last)

    for d in range(2):
        end = 0 if d == 0 else last

        @pl.when(pos[d] == last)
        def _(d=d, end=end):
            add(ex.at[d], [dx.at[end, 1 - x]])
            ex_copy(d).start()

    for k in range(last, 0, -1):
        for a in range(2):
            for d in range(2):
                @pl.when(crosses(d, k, a))
                def _(d=d, k=k, a=a):
                    x_copy(d, k, a).start()
    x_copy(0, 0, 0).start()

    @pl.when(jnp.logical_not(at_end))
    def _():
        x_copy(0, 0, 1).start()

    for copy in loads:
        copy.wait()

    for k in range(last, 0, -1):
        for a in (1, 0):
            gradients(2 * (last - k) + 1 - a)
            for d in range(2):
                @pl.when(pos[d] >= k)
                def _(d=d, k=k, a=a):
                    s = owner(d, k)
                    own = part[a].at[s, x]
                    slot = held.at[a, s]

                    def ready(crossed):
                        if k < last:
                            @pl.when(pos[d] < last)
                            def _():
                                z_in(d, k, a).wait_recv()
                                add(slot, [own, zbuf.at[d, a, s]] + ([slot] if crossed else []))

                        @pl.when(pos[d] == last)
                        def _():
                            add(slot, [own] + ([slot] if crossed else []))

                    if a == 0:
                        x_copy(d, k, a).wait_recv()
                        ready(True)
                    else:
                        @pl.when(pos[d] > k)
                        def _():
                            x_copy(d, k, a).wait_recv()
                            ready(True)

                        @pl.when(pos[d] == k)
                        def _():
                            ready(False)
                    z_copy(d, k, a).start()

        for d in range(2):
            end = 0 if d == 0 else last

            @pl.when(pos[d] == k - 1)
            def _(d=d, end=end, k=k):
                ex_copy(d).wait_recv()
                add(ex.at[d], [ex.at[2 + d], dx.at[end, 1 - x]])
                if k > 1:
                    ex_copy(d).start()
                else:
                    x_copy(0, 0, 1, ex.at[d]).start()

    stores = [
        pltpu.make_async_copy(gate_grad, gate_hbm, store_sem.at[0]),
        pltpu.make_async_copy(up_grad, up_hbm, store_sem.at[1]),
        pltpu.make_async_copy(down_grad, down_hbm, store_sem.at[2]),
    ]
    for copy in stores:
        copy.start()

    for a in range(2):
        x_copy(0, 0, a).wait_recv()
        near = [part[a].at[e, x], held.at[a, e]]

        @pl.when(e < last)
        def _(a=a):
            z_in(0, 0, a).wait_recv()

        @pl.when(e > 0)
        def _(a=a):
            z_in(1, 0, a).wait_recv()

        @pl.when(e == 0)
        def _(a=a, near=near):
            add(outs[a], near + [zbuf.at[0, a, e]])

        @pl.when(e == last)
        def _(a=a, near=near):
            add(outs[a], near + [zbuf.at[1, a, e]])

        @pl.when(jnp.logical_not(at_end))
        def _(a=a, near=near):
            add(outs[a], near + [zbuf.at[0, a, e], zbuf.at[1, a, e]])

    for a in range(2):
        x_copy(0, 0, a).wait_send()
        for k in range(1, levels):
            for d in range(2):
                @pl.when(crosses(d, k, a))
                def _(d=d, k=k, a=a):
                    x_copy(d, k, a).wait_send()

                @pl.when(pos[d] >= k)
                def _(d=d, k=k, a=a):
                    z_copy(d, k, a).wait_send()

    for d in range(2):
        @pl.when(pos[d] > 0)
        def _(d=d):
            ex_copy(d).wait_send()
    for copy in stores:
        copy.wait()


def sems(levels):
    shape = (2, levels + 1, 3)
    return [pltpu.SemaphoreType.DMA(shape)] * 4 + [pltpu.SemaphoreType.DMA((2,))] * 2


def gather_rows(arrays, levels, lines):
    if not by_kernel(arrays[0].shape, levels, lines):
        got = tuple(lax.all_gather(v, ("expert", "dp"), axis=0) for v in arrays)
    else:
        anywhere = pl.BlockSpec(memory_space=pl.ANY)
        got = pl.pallas_call(
            functools.partial(gather_kernel, levels),
            out_shape=tuple(jax.ShapeDtypeStruct((levels, lines) + v.shape, v.dtype) for v in arrays),
            in_specs=[anywhere] * 3,
            out_specs=(anywhere,) * 3,
            scratch_shapes=[pltpu.SemaphoreType.DMA((3,))] + sems(levels),
            compiler_params=pltpu.CompilerParams(collective_id=0, has_side_effects=True),
        )(*arrays)
    return tuple(v.reshape((-1,) + a.shape) for v, a in zip(got, arrays))


def scatter_sums(y_part, dx_part, gate_delta, up_delta, hidden_w, tok, cot, levels, lines):
    width, units = y_part.shape[1], hidden_w.shape[1]
    rows = y_part.shape[0] // (levels * lines)
    low = y_part.dtype
    if not by_kernel((rows, width), levels, lines):
        sums = tuple(
            lax.psum_scatter(v, ("expert", "dp"), scatter_dimension=0, tiled=True) for v in (y_part, dx_part)
        )
        pairs = ((tok, gate_delta), (tok, up_delta), (hidden_w, cot))
        return sums + tuple(contract_first(left, right).astype(low) for left, right in pairs)
    one = jax.ShapeDtypeStruct((rows, width), low)
    tall, wide = (width, units), (units, width)
    vmem = pl.BlockSpec(memory_space=pltpu.VMEM)
    anywhere = pl.BlockSpec(memory_space=pl.ANY)
    return pl.pallas_call(
        functools.partial(scatter_kernel, levels),
        out_shape=(one, one) + tuple(jax.ShapeDtypeStruct(v, low) for v in (tall, tall, wide)),
        in_specs=[vmem] * 5 + [anywhere] * 2,
        out_specs=(vmem,) * 2 + (anywhere,) * 3,
        scratch_shapes=[
            pltpu.VMEM((2, levels, rows, width), low),
            pltpu.VMEM((2, 2, levels, rows, width), low),
            pltpu.VMEM((4, rows, width), low),
            pltpu.VMEM(tok.shape, low),
            pltpu.VMEM(cot.shape, low),
            pltpu.VMEM(tall, low),
            pltpu.VMEM(tall, low),
            pltpu.VMEM(wide, low),
            pltpu.SemaphoreType.DMA((2,)),
            pltpu.SemaphoreType.DMA((3,)),
        ]
        + sems(levels),
        compiler_params=pltpu.CompilerParams(
            collective_id=1, has_side_effects=True, vmem_limit_bytes=VMEM_BYTES
        ),
    )(
        y_part.reshape(levels, lines, rows, width),
        dx_part.reshape(levels, lines, rows, width),
        gate_delta,
        up_delta,
        hidden_w,
        tok,
        cot,
    )


def by_kernel(block, levels, lines):
    rows, width = block
    blocks = 4 * levels * lines + 6 * levels + 14
    return lines == 2 and levels > 2 and rows % CHUNK == 0 and width % TILE == 0 and 2 * blocks * rows * width < VMEM_BYTES


def shards(
    tokens,
    routes,
    route_weight,
    cotangent,
    gate_weight,
    up_weight,
    down_weight,
    pseudo_grad,
    anchor,
    momentum,
):
    axes = ("expert", "dp")
    me = lax.axis_index("expert")
    levels, lines = lax.axis_size("expert"), lax.axis_size("dp")
    meta = jnp.concatenate([routes[0].T.astype(jnp.float32), route_weight[0].T], axis=0)
    meta = jnp.pad(meta, ((0, -meta.shape[0] % 8), (0, 0)))
    tok, cot, meta = gather_rows((tokens[0], cotangent[0], meta), levels, lines)
    tok, cot = tok.reshape(-1, tok.shape[-1]), cot.reshape(-1, cot.shape[-1])
    per_token = routes.shape[-1]
    hit = meta[:, :per_token] == me.astype(jnp.float32)
    weight = jnp.sum(jnp.where(hit, meta[:, per_token : 2 * per_token], 0.0), axis=1).reshape(-1, 1)
    gate_w = gate_weight[0, 0]
    up_w = up_weight[0, 0]
    down_w = down_weight[0, 0]

    gate_pre = jnp.dot(tok, gate_w, preferred_element_type=jnp.float32)
    up_pre = jnp.dot(tok, up_w, preferred_element_type=jnp.float32)
    sig = jax.nn.sigmoid(gate_pre)
    silu_gate = gate_pre * sig
    hidden = silu_gate * up_pre
    hidden_w = (hidden * weight).astype(jnp.bfloat16)
    y_part = jnp.dot(hidden_w, down_w, preferred_element_type=jnp.float32).astype(jnp.bfloat16)

    back = contract_last(cot, down_w)
    mix_rows = jnp.sum(hidden * back, axis=1)
    back_w = back * weight
    gate_delta = (back_w * up_pre * (sig * (1.0 + gate_pre * (1.0 - sig)))).astype(jnp.bfloat16)
    up_delta = (back_w * silu_gate).astype(jnp.bfloat16)
    dx_part = (contract_last(gate_delta, gate_w) + contract_last(up_delta, up_w)).astype(jnp.bfloat16)
    layer_out, token_grad, gate_grad, up_grad, down_grad = scatter_sums(
        y_part, dx_part, gate_delta, up_delta, hidden_w, tok, cot, levels, lines
    )
    mix_part = jnp.where(hit, mix_rows.reshape(hit.shape[0], 1, -1), 0.0)
    mix_part = mix_part.transpose(1, 0, 2).reshape(per_token, -1)
    mix_grad = lax.psum_scatter(mix_part, axes, scatter_dimension=1, tiled=True).T

    island_count = lax.axis_size("replica")
    summed = lax.psum_scatter(
        pseudo_grad[0, 0].astype(jnp.bfloat16), "replica", scatter_dimension=1, tiled=True
    ).astype(jnp.float32)
    mean_grad = summed / island_count
    new_momentum = OUTER_MU * momentum[0] + mean_grad
    new_anchor = anchor[0] - OUTER_RATE * (mean_grad + OUTER_MU * new_momentum)
    return (
        layer_out[None],
        mix_grad[None],
        token_grad[None],
        gate_grad[None, None],
        up_grad[None, None],
        down_grad[None, None],
        new_anchor[None],
        new_momentum[None],
    )


ROWS = P("replica", ("expert", "dp"), None)
COLS = P("replica", "expert", None, "dp")
HIDS = P("replica", "expert", "dp", None)
OUTER = P("expert", "dp", "replica")


def solution(mesh):
    return jax.shard_map(
        shards,
        mesh=mesh,
        in_specs=(ROWS, ROWS, ROWS, ROWS, COLS, COLS, HIDS, HIDS, OUTER, OUTER),
        out_specs=(ROWS, ROWS, ROWS, COLS, COLS, HIDS, OUTER, OUTER),
        check_vma=False,
    )
```

```python
import functools

import jax
import jax.numpy as jnp
from jax import lax
from jax.experimental import pallas as pl
from jax.experimental.pallas import tpu as pltpu
from jax.sharding import PartitionSpec as P

OUTER_MU = 0.9
OUTER_RATE = 0.7


def contract_last(left, right):
    return lax.dot_general(
        left, right, (((1,), (1,)), ((), ())), preferred_element_type=jnp.float32
    )


def contract_first(left, right):
    return lax.dot_general(
        left, right, (((0,), (0,)), ((), ())), preferred_element_type=jnp.float32
    )


MESH = pl.DeviceIdType.MESH
VMEM_BYTES = 58 * 2**20
CHUNK = 16
TILE = 256


def enter(levels):
    e, x = lax.axis_index("expert"), lax.axis_index("dp")
    barrier = pltpu.get_barrier_semaphore()
    pl.semaphore_signal(barrier, inc=1, device_id={"dp": 1 - x}, device_id_type=MESH)

    @pl.when(e > 0)
    def _():
        pl.semaphore_signal(barrier, inc=1, device_id={"expert": e - 1}, device_id_type=MESH)

    @pl.when(e < levels - 1)
    def _():
        pl.semaphore_signal(barrier, inc=1, device_id={"expert": e + 1}, device_id_type=MESH)

    at_end = (e == 0) | (e == levels - 1)

    @pl.when(at_end)
    def _():
        pl.semaphore_wait(barrier, 2)

    @pl.when(jnp.logical_not(at_end))
    def _():
        pl.semaphore_wait(barrier, 3)


def remote(src, dst, sems, device):
    return pltpu.make_async_remote_copy(
        src_ref=src, dst_ref=dst, send_sem=sems[0], recv_sem=sems[1], device_id=device, device_id_type=MESH
    )


def gather_kernel(
    levels, tok, cot, meta, outer, tok_all, cot_all, meta_all, outer_low, outer_in, outer_sem, own_sem, z_send, z_recv, x_send, x_recv, ex_send, ex_recv):
    e, x = lax.axis_index("expert"), lax.axis_index("dp")
    last = levels - 1
    mine, full = (tok, cot, meta), (tok_all, cot_all, meta_all)
    order = (2, 0, 1)
    pos = (e, last - e)
    sign = (-1, 1)
    load = pltpu.make_async_copy(outer, outer_in, outer_sem)
    load.start()
    enter(levels)
    local = [pltpu.make_async_copy(mine[a], full[a].at[e, x], own_sem.at[a]) for a in order]
    for copy in local:
        copy.start()

    def z_copy(d, k, a):
        level = e + sign[d] * (k - 1)
        src = mine[a] if k == 1 else full[a].at[level, x]
        return remote(src, full[a].at[level, x], (z_send.at[d, k, a], z_recv.at[d, k, a]), {"expert": e - sign[d]})

    def z_in(d, k, a):
        level = e + sign[d] * k
        ref = full[a].at[level, x]
        return remote(ref, ref, (z_send.at[d, k, a], z_recv.at[d, k, a]), {"expert": e + sign[d]})

    def x_copy(d, k, a):
        level = e + sign[d] * k
        src = mine[a] if k == 0 else full[a].at[level, x]
        return remote(src, full[a].at[level, x], (x_send.at[d, k, a], x_recv.at[d, k, a]), {"dp": 1 - x})

    def x_in(d, k, a):
        ref = full[a].at[e + sign[d] * k, 1 - x]
        return remote(ref, ref, (x_send.at[d, k, a], x_recv.at[d, k, a]), {"dp": 1 - x})

    def ex_copy(d, go):
        ref = cot_all.at[0 if d == 0 else last, 1 - x]
        return remote(ref, ref, (ex_send.at[d], ex_recv.at[d]), {"expert": e - sign[d] if go else e + sign[d]})

    def crosses(d, k, a):
        return pos[d] > k if a == 1 else pos[d] >= k

    for a in order:
        x_copy(0, 0, a).start()
        for d in range(2):
            @pl.when(pos[d] < last)
            def _(d=d, a=a):
                z_copy(d, 1, a).start()

    load.wait()

    def narrow(i, carry):
        at = pl.ds(pl.multiple_of(i * CHUNK, CHUNK), CHUNK)
        outer_low[at, :] = outer_in[at, :].astype(outer_low.dtype)
        return carry

    lax.fori_loop(0, outer_in.shape[0] // CHUNK, narrow, 0)

    for k in range(1, levels):
        for a in order:
            for d in range(2):
                @pl.when(pos[d] >= k)
                def _(d=d, k=k, a=a):
                    z_in(d, k, a).wait_recv()

                    if k < last:
                        @pl.when(pos[d] < last)
                        def _():
                            z_copy(d, k + 1, a).start()

                @pl.when(crosses(d, k, a))
                def _(d=d, k=k, a=a):
                    x_copy(d, k, a).start()

        if k == 1:
            x_in(0, 0, 1).wait_recv()
            for d in range(2):
                @pl.when(pos[d] == 0)
                def _(d=d):
                    ex_copy(d, True).start()

        for d in range(2):
            @pl.when(pos[d] == k)
            def _(d=d):
                ex_copy(d, False).wait_recv()

                @pl.when(pos[d] < last)
                def _():
                    ex_copy(d, True).start()

    x_in(0, 0, 0).wait_recv()
    x_in(0, 0, 2).wait_recv()
    for a in order:
        x_copy(0, 0, a).wait_send()
    for k in range(1, levels):
        for a in order:
            for d in range(2):
                @pl.when(crosses(d, k, a))
                def _(d=d, k=k, a=a):
                    x_in(d, k, a).wait_recv()
                    x_copy(d, k, a).wait_send()

                @pl.when((pos[d] < last) & (pos[d] >= k - 1))
                def _(d=d, k=k, a=a):
                    z_copy(d, k, a).wait_send()

    for d in range(2):
        @pl.when(pos[d] < last)
        def _(d=d):
            ex_copy(d, True).wait_send()
    for copy in local:
        copy.wait()


def scatter_kernel(
    levels,
    y,
    dx,
    gate_delta,
    up_delta,
    hidden_w,
    tok_hbm,
    cot_hbm,
    y_out,
    dx_out,
    gate_hbm,
    up_hbm,
    down_hbm,
    held,
    zbuf,
    ex,
    tok,
    cot,
    gate_grad,
    up_grad,
    down_grad,
    load_sem,
    store_sem,
    z_send,
    z_recv,
    x_send,
    x_recv,
    ex_send,
    ex_recv,
):
    e, x = lax.axis_index("expert"), lax.axis_index("dp")
    last = levels - 1
    part, outs = (y, dx), (y_out, dx_out)
    pos = (e, last - e)
    sign = (-1, 1)
    rows = y.shape[2]
    loads = [pltpu.make_async_copy(tok_hbm, tok, load_sem.at[0]), pltpu.make_async_copy(cot_hbm, cot, load_sem.at[1])]
    for copy in loads:
        copy.start()
    enter(levels)
    tiles = tok.shape[1] // TILE
    slots = 2 * last

    def contract(left, right):
        return contract_first(left, right).astype(jnp.bfloat16)

    def gradients(slot):
        def body(i, carry):
            at = pl.ds(pl.multiple_of(i * TILE, TILE), TILE)
            gate_grad[at, :] = contract(tok[:, at], gate_delta[...])
            up_grad[at, :] = contract(tok[:, at], up_delta[...])
            down_grad[:, at] = contract(hidden_w[...], cot[:, at])
            return carry

        lax.fori_loop(slot * tiles // slots, (slot + 1) * tiles // slots, body, 0)

    def add(dst, srcs):
        def body(i, carry):
            at = pl.ds(pl.multiple_of(i * CHUNK, CHUNK), CHUNK)
            total = srcs[0][at, :].astype(jnp.float32)
            for src in srcs[1:]:
                total = total + src[at, :].astype(jnp.float32)
            dst[at, :] = total.astype(dst.dtype)
            return carry

        lax.fori_loop(0, rows // CHUNK, body, 0)

    def owner(d, k):
        return e + sign[d] * k

    def x_copy(d, k, a, src=None):
        s = owner(d, k)
        src = part[a].at[s, 1 - x] if src is None else src
        return remote(src, held.at[a, s], (x_send.at[d, k, a], x_recv.at[d, k, a]), {"dp": 1 - x})

    def z_copy(d, k, a):
        s = owner(d, k)
        return remote(held.at[a, s], zbuf.at[d, a, s], (z_send.at[d, k, a], z_recv.at[d, k, a]), {"expert": e + sign[d]})

    def z_in(d, k, a):
        ref = zbuf.at[d, a, owner(d, k)]
        return remote(ref, ref, (z_send.at[d, k + 1, a], z_recv.at[d, k + 1, a]), {"expert": e - sign[d]})

    def ex_copy(d):
        end = 0 if d == 0 else last
        return remote(ex.at[d], ex.at[2 + d], (ex_send.at[d], ex_recv.at[d]), {"expert": e + sign[d]})

    def crosses(d, k, a):
        return pos[d] > k if a == 1 else pos[d] >= k

    at_end = (e == 0) | (e == last)

    for d in range(2):
        end = 0 if d == 0 else last

        @pl.when(pos[d] == last)
        def _(d=d, end=end):
            add(ex.at[d], [dx.at[end, 1 - x]])
            ex_copy(d).start()

    for k in range(last, 0, -1):
        for a in range(2):
            for d in range(2):
                @pl.when(crosses(d, k, a))
                def _(d=d, k=k, a=a):
                    x_copy(d, k, a).start()
    x_copy(0, 0, 0).start()

    @pl.when(jnp.logical_not(at_end))
    def _():
        x_copy(0, 0, 1).start()

    for copy in loads:
        copy.wait()

    for k in range(last, 0, -1):
        for a in (1, 0):
            gradients(2 * (last - k) + 1 - a)
            for d in range(2):
                @pl.when(pos[d] >= k)
                def _(d=d, k=k, a=a):
                    s = owner(d, k)
                    own = part[a].at[s, x]
                    slot = held.at[a, s]

                    def ready(crossed):
                        if k < last:
                            @pl.when(pos[d] < last)
                            def _():
                                z_in(d, k, a).wait_recv()
                                add(slot, [own, zbuf.at[d, a, s]] + ([slot] if crossed else []))

                        @pl.when(pos[d] == last)
                        def _():
                            add(slot, [own] + ([slot] if crossed else []))

                    if a == 0:
                        x_copy(d, k, a).wait_recv()
                        ready(True)
                    else:
                        @pl.when(pos[d] > k)
                        def _():
                            x_copy(d, k, a).wait_recv()
                            ready(True)

                        @pl.when(pos[d] == k)
                        def _():
                            ready(False)
                    z_copy(d, k, a).start()

        for d in range(2):
            end = 0 if d == 0 else last

            @pl.when(pos[d] == k - 1)
            def _(d=d, end=end, k=k):
                ex_copy(d).wait_recv()
                add(ex.at[d], [ex.at[2 + d], dx.at[end, 1 - x]])
                if k > 1:
                    ex_copy(d).start()
                else:
                    x_copy(0, 0, 1, ex.at[d]).start()

    stores = [
        pltpu.make_async_copy(gate_grad, gate_hbm, store_sem.at[0]),
        pltpu.make_async_copy(up_grad, up_hbm, store_sem.at[1]),
        pltpu.make_async_copy(down_grad, down_hbm, store_sem.at[2]),
    ]
    for copy in stores:
        copy.start()

    for a in range(2):
        x_copy(0, 0, a).wait_recv()
        near = [part[a].at[e, x], held.at[a, e]]

        @pl.when(e < last)
        def _(a=a):
            z_in(0, 0, a).wait_recv()

        @pl.when(e > 0)
        def _(a=a):
            z_in(1, 0, a).wait_recv()

        @pl.when(e == 0)
        def _(a=a, near=near):
            add(outs[a], near + [zbuf.at[0, a, e]])

        @pl.when(e == last)
        def _(a=a, near=near):
            add(outs[a], near + [zbuf.at[1, a, e]])

        @pl.when(jnp.logical_not(at_end))
        def _(a=a, near=near):
            add(outs[a], near + [zbuf.at[0, a, e], zbuf.at[1, a, e]])

    for a in range(2):
        x_copy(0, 0, a).wait_send()
        for k in range(1, levels):
            for d in range(2):
                @pl.when(crosses(d, k, a))
                def _(d=d, k=k, a=a):
                    x_copy(d, k, a).wait_send()

                @pl.when(pos[d] >= k)
                def _(d=d, k=k, a=a):
                    z_copy(d, k, a).wait_send()

    for d in range(2):
        @pl.when(pos[d] > 0)
        def _(d=d):
            ex_copy(d).wait_send()
    for copy in stores:
        copy.wait()


def sems(levels):
    shape = (2, levels + 1, 3)
    return [pltpu.SemaphoreType.DMA(shape)] * 4 + [pltpu.SemaphoreType.DMA((2,))] * 2


def gather_rows(arrays, outer, levels, lines):
    if not by_kernel(arrays[0].shape, levels, lines):
        got = tuple(lax.all_gather(v, ("expert", "dp"), axis=0) for v in arrays)
        low = outer.astype(jnp.bfloat16)
    else:
        anywhere = pl.BlockSpec(memory_space=pl.ANY)
        *got, low = pl.pallas_call(
            functools.partial(gather_kernel, levels),
            out_shape=tuple(jax.ShapeDtypeStruct((levels, lines) + v.shape, v.dtype) for v in arrays)
            + (jax.ShapeDtypeStruct(outer.shape, jnp.bfloat16),),
            in_specs=[anywhere] * 4,
            out_specs=(anywhere,) * 3 + (pl.BlockSpec(memory_space=pltpu.VMEM),),
            scratch_shapes=[
                pltpu.VMEM(outer.shape, outer.dtype),
                pltpu.SemaphoreType.DMA,
                pltpu.SemaphoreType.DMA((3,)),
            ]
            + sems(levels),
            compiler_params=pltpu.CompilerParams(collective_id=0, has_side_effects=True, vmem_limit_bytes=VMEM_BYTES),
        )(*arrays, outer)
    return tuple(v.reshape((-1,) + a.shape) for v, a in zip(got, arrays)) + (low,)


def scatter_sums(y_part, dx_part, gate_delta, up_delta, hidden_w, tok, cot, levels, lines):
    width, units = y_part.shape[1], hidden_w.shape[1]
    rows = y_part.shape[0] // (levels * lines)
    low = y_part.dtype
    if not by_kernel((rows, width), levels, lines):
        sums = tuple(
            lax.psum_scatter(v, ("expert", "dp"), scatter_dimension=0, tiled=True) for v in (y_part, dx_part)
        )
        pairs = ((tok, gate_delta), (tok, up_delta), (hidden_w, cot))
        return sums + tuple(contract_first(left, right).astype(low) for left, right in pairs)
    one = jax.ShapeDtypeStruct((rows, width), low)
    tall, wide = (width, units), (units, width)
    vmem = pl.BlockSpec(memory_space=pltpu.VMEM)
    anywhere = pl.BlockSpec(memory_space=pl.ANY)
    return pl.pallas_call(
        functools.partial(scatter_kernel, levels),
        out_shape=(one, one) + tuple(jax.ShapeDtypeStruct(v, low) for v in (tall, tall, wide)),
        in_specs=[vmem] * 5 + [anywhere] * 2,
        out_specs=(vmem,) * 2 + (anywhere,) * 3,
        scratch_shapes=[
            pltpu.VMEM((2, levels, rows, width), low),
            pltpu.VMEM((2, 2, levels, rows, width), low),
            pltpu.VMEM((4, rows, width), low),
            pltpu.VMEM(tok.shape, low),
            pltpu.VMEM(cot.shape, low),
            pltpu.VMEM(tall, low),
            pltpu.VMEM(tall, low),
            pltpu.VMEM(wide, low),
            pltpu.SemaphoreType.DMA((2,)),
            pltpu.SemaphoreType.DMA((3,)),
        ]
        + sems(levels),
        compiler_params=pltpu.CompilerParams(
            collective_id=1, has_side_effects=True, vmem_limit_bytes=VMEM_BYTES
        ),
    )(
        y_part.reshape(levels, lines, rows, width),
        dx_part.reshape(levels, lines, rows, width),
        gate_delta,
        up_delta,
        hidden_w,
        tok,
        cot,
    )


def by_kernel(block, levels, lines):
    rows, width = block
    blocks = 4 * levels * lines + 6 * levels + 14
    return lines == 2 and levels > 2 and rows % CHUNK == 0 and width % TILE == 0 and 2 * blocks * rows * width < VMEM_BYTES


def shards(
    tokens,
    routes,
    route_weight,
    cotangent,
    gate_weight,
    up_weight,
    down_weight,
    pseudo_grad,
    anchor,
    momentum,
):
    axes = ("expert", "dp")
    me = lax.axis_index("expert")
    levels, lines = lax.axis_size("expert"), lax.axis_size("dp")
    meta = jnp.concatenate([routes[0].T.astype(jnp.float32), route_weight[0].T], axis=0)
    meta = jnp.pad(meta, ((0, -meta.shape[0] % 8), (0, 0)))
    tok, cot, meta, outer_low = gather_rows(
        (tokens[0], cotangent[0], meta), pseudo_grad[0, 0], levels, lines
    )
    tok, cot = tok.reshape(-1, tok.shape[-1]), cot.reshape(-1, cot.shape[-1])
    per_token = routes.shape[-1]
    hit = meta[:, :per_token] == me.astype(jnp.float32)
    weight = jnp.sum(jnp.where(hit, meta[:, per_token : 2 * per_token], 0.0), axis=1).reshape(-1, 1)
    gate_w = gate_weight[0, 0]
    up_w = up_weight[0, 0]
    down_w = down_weight[0, 0]

    gate_pre = jnp.dot(tok, gate_w, preferred_element_type=jnp.float32)
    up_pre = jnp.dot(tok, up_w, preferred_element_type=jnp.float32)
    sig = jax.nn.sigmoid(gate_pre)
    silu_gate = gate_pre * sig
    hidden = silu_gate * up_pre
    hidden_w = (hidden * weight).astype(jnp.bfloat16)
    y_part = jnp.dot(hidden_w, down_w, preferred_element_type=jnp.float32).astype(jnp.bfloat16)

    back = contract_last(cot, down_w)
    mix_rows = jnp.sum(hidden * back, axis=1)
    back_w = back * weight
    gate_delta = (back_w * up_pre * (sig * (1.0 + gate_pre * (1.0 - sig)))).astype(jnp.bfloat16)
    up_delta = (back_w * silu_gate).astype(jnp.bfloat16)
    dx_part = (contract_last(gate_delta, gate_w) + contract_last(up_delta, up_w)).astype(jnp.bfloat16)
    layer_out, token_grad, gate_grad, up_grad, down_grad = scatter_sums(
        y_part, dx_part, gate_delta, up_delta, hidden_w, tok, cot, levels, lines
    )
    mix_part = jnp.where(hit, mix_rows.reshape(hit.shape[0], 1, -1), 0.0)
    mix_part = mix_part.transpose(1, 0, 2).reshape(per_token, -1)
    mix_grad = lax.psum_scatter(mix_part, axes, scatter_dimension=1, tiled=True).T

    island_count = lax.axis_size("replica")
    summed = lax.psum_scatter(
        outer_low, "replica", scatter_dimension=1, tiled=True
    ).astype(jnp.float32)
    mean_grad = summed / island_count
    new_momentum = OUTER_MU * momentum[0] + mean_grad
    new_anchor = anchor[0] - OUTER_RATE * (mean_grad + OUTER_MU * new_momentum)
    return (
        layer_out[None],
        mix_grad[None],
        token_grad[None],
        gate_grad[None, None],
        up_grad[None, None],
        down_grad[None, None],
        new_anchor[None],
        new_momentum[None],
    )


ROWS = P("replica", ("expert", "dp"), None)
COLS = P("replica", "expert", None, "dp")
HIDS = P("replica", "expert", "dp", None)
OUTER = P("expert", "dp", "replica")


def solution(mesh):
    return jax.shard_map(
        shards,
        mesh=mesh,
        in_specs=(ROWS, ROWS, ROWS, ROWS, COLS, COLS, HIDS, HIDS, OUTER, OUTER),
        out_specs=(ROWS, ROWS, ROWS, COLS, COLS, HIDS, OUTER, OUTER),
        check_vma=False,
    )
```
